128 devices in a mesh: grp: 16 (over y, x), sp: 8 (over z, core).
Axes of the slice: x: 4, y: 4, z: 4, core: 2. Of those that a mesh axis runs over, the one named last changes fastest.
Arguments:
- clips: bfloat16 [32, 8, 256, 1152], P('grp', None, 'sp'), may hold values from -6 to 6
- counts: int32 [32], replicated, may hold values from 2 to 8, as said below
- dest: int32 [16], replicated, may hold values from 0 to 15, each once
- weight_qkv: bfloat16 [1152, 3456], replicated, may hold values from -0.1875 to 0.1875
- weight_out: bfloat16 [1152, 1152], replicated, may hold values from -0.1875 to 0.1875
- cotangent: bfloat16 [32, 8, 256, 1152], P('grp', None, 'sp'), may hold values from -6 to 6
Outputs:
- outputs: bfloat16 [32, 8, 256, 1152], P('grp', None, 'sp')
- grad_clips: bfloat16 [32, 8, 256, 1152], P('grp', None, 'sp')
The draws below stay inside these ranges and needn't reach their ends.
Inputs may be any that keep to these rules, and one draw needn't show every extreme that they name: `counts`: every clip uses 2 to 8 frames; some clip uses 8 and some uses 2.
All inputs are finite; a program needn't handle non-finite values.
Results may differ from the reference program's by a relative error of at most 0.0065.
Values may be sent and summed in bfloat16 or wider, within the bound.
No kernel may reach another device: no remote copies, remote signals or barrier semaphores. Data moves between devices by JAX's collectives and lax.ppermute only.
A program may use at most 128 MiB of HBM per device.

```python
import jax
import jax.numpy as jnp
from jax import lax

D = 1152
HEADS = 16
HW = 256
FRAMES = 8
CLIPS = 32
N_GRP = 16


def draw_counts(key, part):
    key = jax.random.fold_in(key, 7)
    first, second = jax.random.split(key)
    values = jax.random.randint(first, (CLIPS,), 2, FRAMES + 1).astype(jnp.int32)
    spots = jax.random.permutation(second, CLIPS)
    values = values.at[spots[0]].set(FRAMES).at[spots[1]].set(2)
    return values.astype(jnp.int32)


def levels(own_key, extent, pieces, low, high):
    loudness = 1.0
    for position, parts in pieces:
        steps = jax.random.uniform(jax.random.fold_in(jax.random.fold_in(own_key, 6), position), (parts,), jnp.float32, low / len(pieces), high / len(pieces))
        loudness = loudness * jnp.repeat(jnp.exp(steps), extent[position] // parts).reshape((-1,) + (1,) * (len(extent) - 1 - position))
    return loudness


def centred(stream_key, extent, scale, bound, cuts=(), held_as=jnp.bfloat16):
    drawn = scale * jax.random.normal(stream_key, extent, jnp.float32)
    if cuts:
        drawn = drawn * levels(stream_key, extent, cuts, -0.22, 0.18)
    return jnp.clip(drawn, -bound, bound).astype(held_as)


def setup_inputs(seed: int = 0) -> dict:
    splits = jax.random.split(jax.random.key(seed), 7)
    clips = centred(splits[0], (CLIPS, FRAMES, HW, D), 1.0, 6.0, ((0, 16), (2, 8)))
    counts = draw_counts(jax.random.fold_in(splits[6], 71), 0)
    dest = jax.random.permutation(splits[2], N_GRP).astype(jnp.int32)
    weight_qkv = centred(splits[3], (D, 3 * D), D ** -0.5, 0.1875)
    weight_out = centred(splits[4], (D, D), D ** -0.5, 0.1875)
    cotangent = centred(splits[5], (CLIPS, FRAMES, HW, D), 1.0, 6.0, ((0, 16), (2, 8)))
    return {"clips": clips, "counts": counts, "dest": dest, "weight_qkv": weight_qkv, "weight_out": weight_out, "cotangent": cotangent}


def normed_fn(values):
    mean = lax.optimization_barrier(jnp.mean(values, axis=-1, keepdims=True))
    centered = values - mean
    var = lax.optimization_barrier(jnp.mean(centered * centered, axis=-1, keepdims=True))
    return centered * lax.rsqrt(var + 1e-06)

def attend(query, keys, values):
    scale = query.shape[-1] ** (-0.5)
    scores = jnp.einsum('...qhe,...khe->...hqk', query, keys, preferred_element_type=jnp.float32) * scale
    scores = scores - lax.optimization_barrier(jnp.max(scores, axis=-1, keepdims=True))
    weights = jnp.exp(scores)
    probs = (weights / lax.optimization_barrier(jnp.sum(weights, axis=-1, keepdims=True))).astype(jnp.bfloat16)
    return jnp.einsum('...hqk,...khe->...qhe', probs, values, preferred_element_type=jnp.float32)

def sublayer(tokens, grad_in, used, weight_qkv, weight_out):
    frames, width = (tokens.shape[0], tokens.shape[-1])
    tokens_f = tokens.astype(jnp.float32)
    normed, norm_back = jax.vjp(normed_fn, tokens_f)
    qkv = jnp.dot(normed.astype(jnp.bfloat16), weight_qkv, preferred_element_type=jnp.float32).astype(jnp.bfloat16)
    qkv = qkv.reshape(tokens.shape[:-1] + (3, HEADS, width // HEADS))
    attended, attend_back = jax.vjp(attend, qkv[..., 0, :, :], qkv[..., 1, :, :], qkv[..., 2, :, :])
    attended = attended.astype(jnp.bfloat16).reshape(tokens.shape)
    projected = jnp.dot(attended, weight_out, preferred_element_type=jnp.float32)
    keep = (jnp.arange(frames, dtype=jnp.int32) < used)[:, None, None]
    outputs = jnp.where(keep, tokens_f + projected, 0.0).astype(jnp.bfloat16)
    grad_out = jnp.where(keep, grad_in, jnp.zeros_like(grad_in))
    grad_att = jnp.einsum('fsd,ed->fse', grad_out, weight_out, preferred_element_type=jnp.float32).astype(jnp.bfloat16)
    grad_att = grad_att.reshape(tokens.shape[:-1] + (HEADS, width // HEADS))
    grad_q, grad_k, grad_v = attend_back(grad_att.astype(jnp.float32))
    grad_qkv = jnp.stack([grad_q, grad_k, grad_v], axis=-3).astype(jnp.bfloat16).reshape(tokens.shape[:-1] + (3 * width,))
    grad_norm = jnp.einsum('fse,de->fsd', grad_qkv, weight_qkv, preferred_element_type=jnp.float32)
    grad_work = (grad_out.astype(jnp.float32) + norm_back(grad_norm)[0]).astype(jnp.bfloat16)
    return (outputs, grad_work)

def reference(clips, counts, dest, weight_qkv, weight_out, cotangent):
    groups = dest.shape[0]
    order = jnp.arange(groups, dtype=jnp.int32)
    source = jnp.zeros((groups,), jnp.int32).at[dest].set(order)
    work_from = jnp.stack([2 * order, 2 * source + 1], axis=1).reshape(-1).astype(jnp.int32)
    work = clips[work_from]
    used = counts[work_from]

    def one(items):
        return sublayer(items[0], items[1], items[2], weight_qkv, weight_out)
    outputs, grad_work = lax.map(one, (work, cotangent, used))
    grad_clips = jnp.zeros_like(grad_work).at[work_from].set(grad_work)
    return (outputs, grad_clips)
```

```python
import functools
import jax
import jax.numpy as jnp
from jax import lax
from jax.experimental import pallas as pl
from jax.experimental.pallas import tpu as pltpu
from jax.sharding import PartitionSpec as P

HEADS = 16
HP = 80
GROUPS = 4
EPS = 1e-06
F32 = jnp.float32
BF16 = jnp.bfloat16
LOG2E = 1.4426950408889634
VMEM_LIMIT = 60 * 1024 * 1024


def dot_nn(a, b):
    return lax.dot_general(a, b, (((1,), (0,)), ((), ())), preferred_element_type=F32)


def dot_nt(a, b):
    return lax.dot_general(a, b, (((1,), (1,)), ((), ())), preferred_element_type=F32)


def dot_tn(a, b):
    return lax.dot_general(a, b, (((0,), (0,)), ((), ())), preferred_element_type=F32)


def forward_kernel(scale, x_ref, keep_ref, wt_hbm, wo_hbm, out_ref, qkv_hbm, p_hbm,
                   wt, wo, nrm, qkv, probs, att, wsem, osem, qsem, psem):
    toks = x_ref.shape[0]
    frames = toks // 256
    per = HEADS // GROUPS
    rows = 3 * HP * per

    def weight(g):
        return pltpu.make_async_copy(wt_hbm.at[pl.ds(g * rows, rows)], wt.at[pl.ds(g * rows, rows)], wsem.at[g])

    out_weight = pltpu.make_async_copy(wo_hbm, wo, osem)
    for g in range(GROUPS):
        weight(g).start()
    out_weight.start()
    x = x_ref[...].astype(F32)
    mean = jnp.mean(x, axis=-1, keepdims=True)
    centered = x - mean
    var = jnp.mean(centered * centered, axis=-1, keepdims=True)
    nrm[...] = (centered * lax.rsqrt(var + EPS)).astype(BF16)
    copies = []
    for g in range(GROUPS):
        weight(g).wait()
        part = pl.ds(g * rows, rows)
        qkv[part, :] = dot_nt(wt[part, :], nrm[...]).astype(BF16)
        copy = pltpu.make_async_copy(qkv.at[part], qkv_hbm.at[part], qsem.at[g])
        copy.start()
        copies.append(copy)
        for h in range(g * per, (g + 1) * per):
            for f in range(frames):
                cols = pl.ds(f * 256, 256)
                q = qkv[pl.ds(3 * HP * h, HP), cols]
                k = qkv[pl.ds(3 * HP * h + HP, HP), cols]
                v = qkv[pl.ds(3 * HP * h + 2 * HP, HP), cols]
                s = dot_tn(k, q)
                top = jnp.max(s, axis=0, keepdims=True)
                e = jnp.exp2((s - top) * (scale * LOG2E))
                p = (e * (1.0 / jnp.sum(e, axis=0, keepdims=True))).astype(BF16)
                probs[h, :, cols] = p
                att[pl.ds(HP * h, HP), cols] = dot_nn(v, p).astype(BF16)
        part = pl.ds(g * per, per)
        copy = pltpu.make_async_copy(probs.at[part], p_hbm.at[part], psem.at[g])
        copy.start()
        copies.append(copy)
    out_weight.wait()
    projected = dot_tn(att[...], wo[...])
    out_ref[...] = jnp.where(keep_ref[...] > 0, x_ref[...].astype(F32) + projected, 0.0).astype(BF16)
    for copy in copies:
        copy.wait()


def forward(x, keep, wt, wo, scale):
    toks, width = x.shape
    return pl.pallas_call(
        functools.partial(forward_kernel, scale),
        out_shape=(
            jax.ShapeDtypeStruct((toks, width), BF16),
            jax.ShapeDtypeStruct((wt.shape[0], toks), BF16),
            jax.ShapeDtypeStruct((HEADS, 256, toks), BF16),
        ),
        in_specs=[pl.BlockSpec(memory_space=pltpu.VMEM)] * 2 + [pl.BlockSpec(memory_space=pl.ANY)] * 2,
        out_specs=(pl.BlockSpec(memory_space=pltpu.VMEM), pl.BlockSpec(memory_space=pl.ANY), pl.BlockSpec(memory_space=pl.ANY)),
        scratch_shapes=[
            pltpu.VMEM(wt.shape, BF16),
            pltpu.VMEM(wo.shape, BF16),
            pltpu.VMEM((toks, width), BF16),
            pltpu.VMEM((wt.shape[0], toks), BF16),
            pltpu.VMEM((HEADS, 256, toks), BF16),
            pltpu.VMEM((wo.shape[0], toks), BF16),
            pltpu.SemaphoreType.DMA((GROUPS,)),
            pltpu.SemaphoreType.DMA,
            pltpu.SemaphoreType.DMA((GROUPS,)),
            pltpu.SemaphoreType.DMA((GROUPS,)),
        ],
        compiler_params=pltpu.CompilerParams(vmem_limit_bytes=VMEM_LIMIT),
        name="forward",
    )(x, keep, wt, wo)


def backward_kernel(scale, x_ref, c_ref, keep_ref, wt_hbm, wo_hbm, qkv_hbm, p_hbm, out_ref,
                    wt, wo, qkv, probs, gatt, gqkv, wsem, osem, qsem, psem):
    toks = x_ref.shape[0]
    frames = toks // 256
    per = HEADS // GROUPS
    rows = 3 * HP * per

    def load_qkv(g):
        part = pl.ds(g * rows, rows)
        return pltpu.make_async_copy(qkv_hbm.at[part], qkv.at[part], qsem.at[g])

    def load_probs(g):
        part = pl.ds(g * per, per)
        return pltpu.make_async_copy(p_hbm.at[part], probs.at[part], psem.at[g])

    load_wo = pltpu.make_async_copy(wo_hbm, wo, osem)
    load_wt = pltpu.make_async_copy(wt_hbm, wt, wsem)
    load_wo.start()
    for g in range(GROUPS):
        load_qkv(g).start()
        load_probs(g).start()
    load_wt.start()
    keep = keep_ref[...] > 0
    gout = jnp.where(keep, c_ref[...], jnp.zeros_like(c_ref[...]))
    load_wo.wait()
    gatt[...] = dot_nt(wo[...], gout).astype(BF16)
    for g in range(GROUPS):
        load_qkv(g).wait()
        load_probs(g).wait()
        for h in range(g * per, (g + 1) * per):
            for f in range(frames):
                cols = pl.ds(f * 256, 256)
                at = 3 * HP * h
                q = qkv[pl.ds(at, HP), cols]
                k = qkv[pl.ds(at + HP, HP), cols]
                v = qkv[pl.ds(at + 2 * HP, HP), cols]
                p = probs[h, :, cols]
                ga = gatt[pl.ds(HP * h, HP), cols]
                gp = dot_tn(v, ga)
                pf = p.astype(F32)
                mass = jnp.sum(pf * gp, axis=0, keepdims=True)
                gs = (pf * (gp - mass) * scale).astype(BF16)
                gqkv[pl.ds(at, HP), cols] = dot_nn(k, gs).astype(BF16)
                gqkv[pl.ds(at + HP, HP), cols] = dot_nt(q, gs).astype(BF16)
                gqkv[pl.ds(at + 2 * HP, HP), cols] = dot_nt(ga, p).astype(BF16)
    load_wt.wait()
    gn = dot_tn(gqkv[...], wt[...])
    x = x_ref[...].astype(F32)
    mean = jnp.mean(x, axis=-1, keepdims=True)
    centered = x - mean
    var = jnp.mean(centered * centered, axis=-1, keepdims=True)
    inv = lax.rsqrt(var + EPS)
    n = centered * inv
    gx = inv * (gn - jnp.mean(gn, axis=-1, keepdims=True) - n * jnp.mean(gn * n, axis=-1, keepdims=True))
    gout = jnp.where(keep, c_ref[...], jnp.zeros_like(c_ref[...])).astype(F32)
    out_ref[...] = (gout + gx).astype(BF16)


def backward(x, c, keep, wt, wo, qkv, probs, scale):
    toks, width = x.shape
    return pl.pallas_call(
        functools.partial(backward_kernel, scale),
        out_shape=jax.ShapeDtypeStruct((toks, width), BF16),
        in_specs=[pl.BlockSpec(memory_space=pltpu.VMEM)] * 3 + [pl.BlockSpec(memory_space=pl.ANY)] * 4,
        out_specs=pl.BlockSpec(memory_space=pltpu.VMEM),
        scratch_shapes=[
            pltpu.VMEM(wt.shape, BF16),
            pltpu.VMEM(wo.shape, BF16),
            pltpu.VMEM(qkv.shape, BF16),
            pltpu.VMEM(probs.shape, BF16),
            pltpu.VMEM((wo.shape[0], toks), BF16),
            pltpu.VMEM(qkv.shape, BF16),
            pltpu.SemaphoreType.DMA,
            pltpu.SemaphoreType.DMA,
            pltpu.SemaphoreType.DMA((GROUPS,)),
            pltpu.SemaphoreType.DMA((GROUPS,)),
        ],
        compiler_params=pltpu.CompilerParams(vmem_limit_bytes=VMEM_LIMIT),
        name="backward",
    )(x, c, keep, wt, wo, qkv, probs)


def pad_weights(weight_qkv, weight_out):
    width = weight_out.shape[0]
    hd = width // HEADS
    wt = weight_qkv.T.reshape(3, HEADS, hd, width).transpose(1, 0, 2, 3)
    wt = jnp.pad(wt, ((0, 0), (0, 0), (0, HP - hd), (0, 0))).reshape(HEADS * 3 * HP, width)
    wo = jnp.pad(weight_out.reshape(HEADS, hd, width), ((0, 0), (0, HP - hd), (0, 0))).reshape(HEADS * HP, width)
    return wt, wo


def shuffle_kernel(index_ref, x_hbm, out_hbm, sem):
    copies = [
        pltpu.make_async_copy(x_hbm.at[index_ref[i]], out_hbm.at[i], sem.at[i]) for i in range(x_hbm.shape[0])
    ]
    for copy in copies:
        copy.start()
    for copy in copies:
        copy.wait()


def shuffle(x, index):
    return pl.pallas_call(
        shuffle_kernel,
        out_shape=jax.ShapeDtypeStruct(x.shape, x.dtype),
        in_specs=[pl.BlockSpec(memory_space=pltpu.SMEM), pl.BlockSpec(memory_space=pl.ANY)],
        out_specs=pl.BlockSpec(memory_space=pl.ANY),
        scratch_shapes=[pltpu.SemaphoreType.DMA((x.shape[0],))],
        name="shuffle",
    )(index, x)


def route(x, index, groups):
    tokens, width = x.shape
    pieces = x.reshape(groups, tokens // groups, width)
    pieces = lax.all_to_all(pieces, "grp", 0, 0, tiled=True)
    pieces = shuffle(pieces, index)
    pieces = lax.all_to_all(pieces, "grp", 0, 0, tiled=True)
    return pieces.reshape(tokens, width)


def gather_frame(x):
    frames, part, width = x.shape
    return lax.all_to_all(x, "sp", 0, 0, tiled=True).reshape(frames * part, width)


def scatter_frame(x, frames):
    tokens, width = x.shape
    return lax.all_to_all(x.reshape(frames, tokens // frames, width), "sp", 0, 0, tiled=True)


def on_device(clips, counts, dest, weight_qkv, weight_out, cotangent):
    groups = lax.axis_size("grp")
    me = lax.axis_index("grp")
    frame = lax.axis_index("sp")
    frames = clips.shape[1]
    order = jnp.arange(groups, dtype=jnp.int32)
    source = jnp.sum(jnp.where(dest[None, :] == order[:, None], order[None, :], 0), axis=1)
    scale = (weight_out.shape[0] // HEADS) ** -0.5
    wt, wo = pad_weights(weight_qkv, weight_out)
    xa = gather_frame(clips[0])
    xb = gather_frame(clips[1])
    ca = gather_frame(cotangent[0])
    cb = route(gather_frame(cotangent[1]), dest, groups)
    x = jnp.concatenate([xa, xb])
    c = jnp.concatenate([ca, cb])
    used = lax.dynamic_slice_in_dim(counts, 2 * me, 2)
    keep = jnp.repeat((frame < used).astype(F32), 256)[:, None]
    out, qkv, probs = forward(x, keep, wt, wo, scale)
    grad = backward(x, c, keep, wt, wo, qkv, probs, scale)
    oa = scatter_frame(out[:256], frames)
    ob = scatter_frame(route(out[256:], source, groups), frames)
    ga = scatter_frame(grad[:256], frames)
    gb = scatter_frame(grad[256:], frames)
    return (jnp.stack([oa, ob]), jnp.stack([ga, gb]))


def solution(mesh):
    spec = P("grp", None, "sp", None)
    return jax.shard_map(
        on_device, mesh=mesh, in_specs=(spec, P(), P(), P(), P(), spec), out_specs=(spec, spec), check_vma=False
    )
```

```python
import functools
import jax
import jax.numpy as jnp
from jax import lax
from jax.experimental import pallas as pl
from jax.experimental.pallas import tpu as pltpu
from jax.sharding import PartitionSpec as P

HEADS = 16
HP = 80
GROUPS = 4
EPS = 1e-06
F32 = jnp.float32
BF16 = jnp.bfloat16
LOG2E = 1.4426950408889634
MIB = 1024 * 1024
IN_VMEM = pl.BlockSpec(memory_space=pltpu.VMEM)
IN_SMEM = pl.BlockSpec(memory_space=pltpu.SMEM)
ANYWHERE = pl.BlockSpec(memory_space=pltpu.HBM)


def dot_nn(a, b):
    return lax.dot_general(a, b, (((1,), (0,)), ((), ())), preferred_element_type=F32)


def dot_nt(a, b):
    return lax.dot_general(a, b, (((1,), (1,)), ((), ())), preferred_element_type=F32)


def dot_tn(a, b):
    return lax.dot_general(a, b, (((0,), (0,)), ((), ())), preferred_element_type=F32)


def cost(flops, moved):
    return pl.CostEstimate(flops=flops, bytes_accessed=moved, transcendentals=0)


def far(x):
    return pltpu.with_memory_space_constraint(x, pltpu.HBM)


def copy_all(pairs, sems):
    copies = [pltpu.make_async_copy(src, dst, sems.at[n]) for n, (src, dst) in enumerate(pairs)]
    for copy in copies:
        copy.start()
    return copies


def wait_all(copies):
    for copy in copies:
        copy.wait()


def prepare_kernel(wq_hbm, wo_hbm, wt_hbm, wop_hbm, wt_ref, wop_ref, out_sems, wq, wo, sems):
    width = wo.shape[0]
    hd = width // HEADS
    loads = [
        pltpu.make_async_copy(wq_hbm.at[:, pl.ds(j * width, width)], wq.at[j], sems.at[j]) for j in range(3)
    ]
    loads.append(pltpu.make_async_copy(wo_hbm, wo, sems.at[3]))
    for load in loads:
        load.start()
    pad = jnp.zeros((HP - hd, width), F32)

    def put(dst, rows, j):
        for h in range(HEADS):
            part = jnp.concatenate([rows[h * hd:(h + 1) * hd], pad])
            dst[pl.ds((j * HEADS + h) * HP, HP), :] = part.astype(BF16)

    saves = []
    for j in range(3):
        loads[j].wait()
        put(wt_ref, wq[j].astype(F32).T, j)
        part = pl.ds(j * HEADS * HP, HEADS * HP)
        saves.append(pltpu.make_async_copy(wt_ref.at[part], wt_hbm.at[part], out_sems.at[j]))
        saves[-1].start()
    loads[3].wait()
    put(wop_ref, wo[...].astype(F32), 0)
    saves.append(pltpu.make_async_copy(wop_ref, wop_hbm, out_sems.at[3]))
    saves[-1].start()
    wait_all(saves)


def prepare(weight_qkv, weight_out):
    width = weight_out.shape[0]
    return pl.pallas_call(
        prepare_kernel,
        out_shape=(pltpu.HBM((3 * HEADS * HP, width), BF16), pltpu.HBM((HEADS * HP, width), BF16)),
        in_specs=[ANYWHERE] * 2,
        out_specs=(ANYWHERE, ANYWHERE),
        scratch_shapes=[
            pltpu.VMEM((3 * HEADS * HP, width), BF16),
            pltpu.VMEM((HEADS * HP, width), BF16),
            pltpu.SemaphoreType.DMA((4,)),
            pltpu.VMEM((3, width, width), BF16),
            pltpu.VMEM((width, width), BF16),
            pltpu.SemaphoreType.DMA((4,)),
        ],
        compiler_params=pltpu.CompilerParams(vmem_limit_bytes=40 * MIB),
        name="prepare",
    )(far(weight_qkv), far(weight_out))


def assemble(dst, f, own, part_of, pieces, from_ref, sems):
    count = sems.shape[1]
    part = own.shape[1]
    copies = []
    for n in range(count):
        if pieces:
            at = from_ref[n]
            src = pieces[n - 1].at[part_of] if n else own.at[at]
        else:
            at = n
            src = own.at[n]
        copies.append(pltpu.make_async_copy(src, dst.at[pl.ds(f * count * part + at * part, part)], sems.at[f, n]))
    for copy in copies:
        copy.start()
    return copies


def forward_kernel(scale, from_ref, keep_ref, wt_hbm, wo_hbm, clips, *rest):
    pieces, (out_a, out_b, x_hbm, qkv_hbm, p_hbm, inverse) = rest[:-19], rest[-19:-13]
    nrm, att, sbuf, sems, x_ref, qkv, probs, wt, wo, total, wsem, osem, ssem = rest[-13:]
    copies = []
    for f in range(2):
        copies += assemble(x_ref, f, clips.at[f], f, pieces, from_ref, sems)
    first = HP * HEADS // GROUPS
    parts = [pl.ds(j * HEADS * HP, first) for j in range(3)]
    parts += [pl.ds(j * HEADS * HP + first, HEADS * HP - first) for j in range(3)]
    weights = copy_all([(wt_hbm.at[part], wt.at[part]) for part in parts], wsem)
    out_weight = copy_all([(wo_hbm, wo)], osem)
    wait_all(copies)
    toks = x_ref.shape[0]
    frames = toks // 256
    per = HEADS // GROUPS
    rows = HP * per
    third = HEADS * HP
    x = x_ref[...].astype(F32)
    mean = jnp.mean(x, axis=-1, keepdims=True)
    centered = x - mean
    var = jnp.mean(centered * centered, axis=-1, keepdims=True)
    nrm[...] = (centered * lax.rsqrt(var + EPS)).astype(BF16)
    units = [(h, f) for h in range(HEADS) for f in range(frames)]

    def project(g):
        for j in range(3):
            part = pl.ds(j * third + g * rows, rows)
            qkv[part, :] = dot_nt(wt[part, :], nrm[...]).astype(BF16)

    def scores(i):
        h, f = units[i]
        cols = pl.ds(f * 256, 256)
        q = qkv[pl.ds(HP * h, HP), cols]
        k = qkv[pl.ds(third + HP * h, HP), cols]
        sbuf[i % 2] = dot_tn(k, q)

    def soften(i):
        h, f = units[i]
        s = sbuf[i % 2]
        top = jnp.max(s, axis=0, keepdims=True)
        e = jnp.exp2((s - top) * (scale * LOG2E))
        probs[h, :, pl.ds(f * 256, 256)] = e.astype(BF16)
        inv = 1.0 / jnp.sum(e, axis=0, keepdims=True)
        inverse[h, :, pl.ds(f * 256, 256)] = inv

    def mix(i):
        h, f = units[i]
        cols = pl.ds(f * 256, 256)
        v = qkv[pl.ds(2 * third + HP * h, HP), cols]
        att[pl.ds(HP * h, HP), cols] = (dot_nn(v, probs[h, :, cols]) * inverse[h, :, cols]).astype(BF16)

    wait_all(weights[:3])
    project(0)
    wait_all(weights[3:])
    scores(0)
    for i in range(len(units)):
        h, f = units[i]
        if f == 0 and h % per == per - 2 and h // per + 1 < GROUPS:
            project(h // per + 1)
        if f == 0 and h == HEADS // 2 + 1:
            half = pl.ds(0, HEADS // 2)
            saves = [pltpu.make_async_copy(probs.at[half], p_hbm.at[half], ssem.at[0])]
            saves[-1].start()
        if f == 0 and h == HEADS - per:
            saves += [
                pltpu.make_async_copy(qkv, qkv_hbm, ssem.at[1]),
                pltpu.make_async_copy(x_ref, x_hbm, ssem.at[2]),
            ]
            saves[-1].start()
            saves[-2].start()
        if i + 1 < len(units):
            scores(i + 1)
        soften(i)
        if i:
            mix(i - 1)
    mix(len(units) - 1)
    half = pl.ds(HEADS // 2, HEADS // 2)
    saves.append(pltpu.make_async_copy(probs.at[half], p_hbm.at[half], ssem.at[3]))
    saves[-1].start()
    wait_all(out_weight)
    projected = dot_tn(att[...], wo[...])
    total[...] = (x_ref[...].astype(F32) + projected).astype(BF16)
    for f, out_ref in enumerate((out_a, out_b)):
        part = pl.ds(f * 256, 256)

        @pl.when(keep_ref[f] == 0)
        def _():
            total[part] = jnp.zeros((256, total.shape[1]), BF16)

        saves.append(pltpu.make_async_copy(total.at[part], out_ref, ssem.at[4 + f]))
        saves[-1].start()
    wait_all(saves)


def forward(clips, pieces, origins, keep, wt, wo, scale):
    frames, part, width = clips.shape[1:]
    toks = frames * part
    out = pltpu.HBM((toks, width), BF16)
    return pl.pallas_call(
        functools.partial(forward_kernel, scale),
        out_shape=(
            out,
            out,
            pltpu.HBM((2 * toks, width), BF16),
            pltpu.HBM((wt.shape[0], 2 * toks), BF16),
            pltpu.HBM((HEADS, toks, 2 * toks), BF16),
            jax.ShapeDtypeStruct((HEADS, 1, 2 * toks), F32),
        ),
        in_specs=[IN_SMEM] * 2 + [ANYWHERE] * (3 + len(pieces)),
        out_specs=(ANYWHERE,) * 5 + (IN_VMEM,),
        scratch_shapes=[
            pltpu.VMEM((2 * toks, width), BF16),
            pltpu.VMEM((wo.shape[0], 2 * toks), BF16),
            pltpu.VMEM((2, toks, toks), F32),
            pltpu.SemaphoreType.DMA((2, frames)),
            pltpu.VMEM((2 * toks, width), BF16),
            pltpu.VMEM((wt.shape[0], 2 * toks), BF16),
            pltpu.VMEM((HEADS, toks, 2 * toks), BF16),
            pltpu.VMEM(wt.shape, BF16),
            pltpu.VMEM(wo.shape, BF16),
            pltpu.VMEM((2 * toks, width), BF16),
            pltpu.SemaphoreType.DMA((6,)),
            pltpu.SemaphoreType.DMA((1,)),
            pltpu.SemaphoreType.DMA((6,)),
        ],
        compiler_params=pltpu.CompilerParams(vmem_limit_bytes=48 * MIB),
        cost_estimate=cost(4 * toks * (wt.size + wo.size) + 8 * wo.shape[0] * toks * toks, 2 * (wt.size + wo.size)),
        name="forward",
    )(origins, keep, far(wt), far(wo), far(clips), *[far(x) for x in pieces])


def backward_kernel(scale, from_ref, keep_ref, inverse, wt_hbm, wo_hbm, x_hbm, qkv_hbm, p_hbm, cot_a, cot_b, *rest):
    pieces, (ga_ref, gb_ref, c_ref, gatt, gqkv, gabuf, gpbuf, gsbuf, sems) = rest[:-16], rest[-16:-7]
    x_ref, qkv, probs, wt, wo, total, lsem = rest[-7:]
    copies = assemble(c_ref, 0, cot_a, 2, pieces, from_ref, sems) + assemble(c_ref, 1, cot_b, 0, [], from_ref, sems)
    low, high = pl.ds(0, HEADS // 2), pl.ds(HEADS // 2, HEADS // 2)
    pairs = [(wo_hbm, wo), (qkv_hbm, qkv), (p_hbm.at[low], probs.at[low]), (p_hbm.at[high], probs.at[high])]
    loads = copy_all(pairs + [(x_hbm, x_ref), (wt_hbm, wt)], lsem)
    wait_all(copies)
    for f in range(2):
        part = c_ref[pl.ds(f * 256, 256)]
        c_ref[pl.ds(f * 256, 256)] = jnp.where(keep_ref[f] > 0, part, jnp.zeros_like(part))
    toks = x_ref.shape[0]
    frames = toks // 256
    third = HEADS * HP
    wait_all(loads[:1])
    gatt[...] = dot_nt(wo[...], c_ref[...])
    wait_all(loads[1:3])
    units = [(h, f) for h in range(HEADS) for f in range(frames)]

    def rows_of(h):
        return [pl.ds(j * third + HP * h, HP) for j in range(3)]

    def reach(i):
        h, f = units[i]
        cols = pl.ds(f * 256, 256)
        part = pl.ds(HP * h, HP)
        ga = (gatt[part, cols] * inverse[h, :, cols]).astype(BF16)
        gabuf[i % 2] = ga
        gpbuf[i % 2] = dot_tn(qkv[rows_of(h)[2], cols], ga)

    def soften(i):
        h, f = units[i]
        cols = pl.ds(f * 256, 256)
        gp = gpbuf[i % 2]
        e = probs[h, :, cols].astype(F32)
        mass = jnp.sum(e * gp, axis=0, keepdims=True) * inverse[h, :, cols]
        gsbuf[i % 2] = (e * (gp - mass) * scale).astype(BF16)

    def spread(i):
        h, f = units[i]
        cols = pl.ds(f * 256, 256)
        at = rows_of(h)
        gs = gsbuf[i % 2]
        gqkv[at[0], cols] = dot_nn(qkv[at[1], cols], gs).astype(BF16)
        gqkv[at[1], cols] = dot_nt(qkv[at[0], cols], gs).astype(BF16)

    def values(i):
        h, f = units[i]
        cols = pl.ds(f * 256, 256)
        gqkv[rows_of(h)[2], cols] = dot_nt(gabuf[i % 2], probs[h, :, cols]).astype(BF16)

    reach(0)
    for i in range(len(units)):
        if units[i] == (HEADS // 2, 0):
            wait_all(loads[3:4])
        values(i)
        if i + 1 < len(units):
            reach(i + 1)
        soften(i)
        if i:
            spread(i - 1)
    spread(len(units) - 1)
    wait_all(loads[4:])
    gn = dot_tn(gqkv[...], wt[...])
    x = x_ref[...].astype(F32)
    mean = jnp.mean(x, axis=-1, keepdims=True)
    centered = x - mean
    var = jnp.mean(centered * centered, axis=-1, keepdims=True)
    inv = lax.rsqrt(var + EPS)
    n = centered * inv
    gx = inv * (gn - jnp.mean(gn, axis=-1, keepdims=True) - n * jnp.mean(gn * n, axis=-1, keepdims=True))
    total[...] = (c_ref[...].astype(F32) + gx).astype(BF16)
    wait_all(copy_all([(total.at[pl.ds(0, 256)], ga_ref), (total.at[pl.ds(256, 256)], gb_ref)], lsem))


def backward(cot_a, cot_b, pieces, origins, keep, wt, wo, kept, scale):
    frames, part, width = cot_a.shape
    toks = frames * part
    x, qkv, probs, inverse = kept
    out = pltpu.HBM((toks, width), BF16)
    return pl.pallas_call(
        functools.partial(backward_kernel, scale),
        out_shape=(out, out),
        in_specs=[IN_SMEM] * 2 + [IN_VMEM] + [ANYWHERE] * (7 + len(pieces)),
        out_specs=(ANYWHERE, ANYWHERE),
        scratch_shapes=[
            pltpu.VMEM((2 * toks, width), BF16),
            pltpu.VMEM((wo.shape[0], 2 * toks), F32),
            pltpu.VMEM(qkv.shape, BF16),
            pltpu.VMEM((2, HP, toks), BF16),
            pltpu.VMEM((2, toks, toks), F32),
            pltpu.VMEM((2, toks, toks), BF16),
            pltpu.SemaphoreType.DMA((2, frames)),
            pltpu.VMEM(x.shape, BF16),
            pltpu.VMEM(qkv.shape, BF16),
            pltpu.VMEM(probs.shape, BF16),
            pltpu.VMEM(wt.shape, BF16),
            pltpu.VMEM(wo.shape, BF16),
            pltpu.VMEM(x.shape, BF16),
            pltpu.SemaphoreType.DMA((6,)),
        ],
        compiler_params=pltpu.CompilerParams(vmem_limit_bytes=48 * MIB),
        cost_estimate=cost(4 * toks * (wt.size + wo.size) + 16 * wo.shape[0] * toks * toks, 2 * (wt.size + wo.size)),
        name="backward",
    )(origins, keep, inverse, *[far(x) for x in (wt, wo, x, qkv, probs, cot_a, cot_b)], *[far(x) for x in pieces])


def shuffle_kernel(index_ref, x_ref, out_ref):
    for i in range(x_ref.shape[0]):
        out_ref[i] = x_ref[index_ref[i]]


def shuffle(x, index):
    return pl.pallas_call(
        shuffle_kernel,
        out_shape=jax.ShapeDtypeStruct(x.shape, x.dtype),
        in_specs=[IN_SMEM, IN_VMEM],
        out_specs=IN_VMEM,
        compiler_params=pltpu.CompilerParams(vmem_limit_bytes=8 * MIB),
        name="shuffle",
    )(index, x)


def spread(x, groups):
    return lax.all_to_all(x.reshape(groups, -1, x.shape[-1]), "grp", 0, 0, tiled=True)


def pack_kernel(leads, to_ref, *refs):
    count = len(leads)
    sources, outs, sems = refs[:count], refs[count:-1], refs[-1]
    copies = []
    for n, out in enumerate(outs):
        at = to_ref[n + 1]
        for a, lead in enumerate(leads):
            src = sources[a] if lead is None else sources[a].at[lead[0]]
            copies.append(pltpu.make_async_copy(src.at[at], out.at[a], sems.at[n, a]))
    for copy in copies:
        copy.start()
    for copy in copies:
        copy.wait()


def pack(sources, leads, targets):
    n = targets.shape[0]
    block = sources[0].shape[-2:]
    return pl.pallas_call(
        functools.partial(pack_kernel, leads),
        out_shape=(jax.ShapeDtypeStruct((len(leads),) + block, BF16),) * (n - 1),
        in_specs=[IN_SMEM] + [ANYWHERE] * len(sources),
        out_specs=(IN_VMEM,) * (n - 1),
        scratch_shapes=[pltpu.SemaphoreType.DMA((n - 1, len(leads)))],
        compiler_params=pltpu.CompilerParams(vmem_limit_bytes=12 * MIB),
        name="pack",
    )(targets, *[far(x) for x in sources])


def unpack_kernel(picks, from_ref, *refs):
    owns = len(picks)
    sources, (out, held, in_sems, out_sems) = refs[:-4], refs[-4:]
    own, pieces = sources[:owns], sources[owns:]
    reads, writes = [], []
    for a, pick in enumerate(picks):
        for n in range(in_sems.shape[1]):
            at = from_ref[n]
            first, clip = pick
            src = pieces[first + n - 1].at[clip] if n else own[a].at[at]
            reads.append(pltpu.make_async_copy(src, held.at[a, n], in_sems.at[a, n]))
            writes.append(pltpu.make_async_copy(held.at[a, n], out.at[a, at], out_sems.at[a, n]))
    for read in reads:
        read.start()
    for read, write in zip(reads, writes):
        read.wait()
        write.start()
    wait_all(writes)


def unpack(own, pieces, picks, origins):
    n = origins.shape[0]
    shape = (len(picks),) + own[0].shape
    return pl.pallas_call(
        functools.partial(unpack_kernel, picks),
        out_shape=pltpu.HBM(shape, BF16),
        in_specs=[IN_SMEM] + [ANYWHERE] * (len(own) + len(pieces)),
        out_specs=ANYWHERE,
        scratch_shapes=[
            pltpu.VMEM(shape, BF16),
            pltpu.SemaphoreType.DMA((len(picks), n)),
            pltpu.SemaphoreType.DMA((len(picks), n)),
        ],
        compiler_params=pltpu.CompilerParams(vmem_limit_bytes=12 * MIB),
        name="unpack",
    )(origins, *[far(x) for x in own], *[far(x) for x in pieces])


def exchange(sends, size):
    chips = size // 2
    out = []
    for n, x in enumerate(sends, start=1):
        pairs = [(i, (i // 2 + n // 2) % chips * 2 + (i % 2 ^ n % 2)) for i in range(size)]
        out.append(lax.ppermute(x, "sp", pairs))
    return out


def settle(pieces, *others):
    across = [n for n in range(len(pieces)) if (n + 1) // 2 == (len(pieces) + 1) // 4]
    near = [n for n in range(len(pieces)) if n not in across]
    *held, rest = lax.optimization_barrier((*[pieces[n] for n in near], others))
    pieces = list(pieces)
    for n, piece in zip(near, held):
        pieces[n] = piece
    return (pieces, *rest)


def on_device(clips, counts, dest, weight_qkv, weight_out, cotangent):
    groups = lax.axis_size("grp")
    size = lax.axis_size("sp")
    me = lax.axis_index("grp")
    frame = lax.axis_index("sp")
    order = jnp.arange(groups, dtype=jnp.int32)
    source = jnp.sum(jnp.where(dest[None, :] == order[:, None], order[None, :], 0), axis=1)
    offset = jnp.arange(size, dtype=jnp.int32)
    targets = (frame // 2 + offset // 2) % (size // 2) * 2 + (frame + offset) % 2
    origins = (frame // 2 - offset // 2) % (size // 2) * 2 + (frame + offset) % 2
    scale = (weight_out.shape[0] // HEADS) ** -0.5
    used = lax.dynamic_slice_in_dim(counts, 2 * me, 2)
    keep = (frame < used).astype(jnp.int32)
    keep_a, keep_b = keep[0:1], keep[1:2]

    block = clips.shape[1:]
    cot_b = spread(cotangent[1], groups)
    pieces = exchange(pack((clips, clips, cotangent), ((0,), (1,), (0,)), targets), size)
    wt, wo = prepare(weight_qkv, weight_out)
    pieces, cot_b, wt = settle(pieces, cot_b, wt)
    cot_b = spread(shuffle(cot_b, dest), groups).reshape(block)
    cot_b, wt = lax.optimization_barrier((cot_b, wt))
    out_a, out_b, *kept = forward(clips, pieces, origins, keep, wt, wo, scale)
    cot_b = lax.all_to_all(cot_b, "sp", 0, 0, tiled=True)
    cot_b, out_b = lax.optimization_barrier((cot_b, out_b))
    out_b = spread(out_b, groups)
    grad_a, grad_b = backward(cotangent[0], cot_b, pieces, origins, keep, wt, wo, kept, scale)
    grad_a, grad_b, out_a = grad_a.reshape(block), grad_b.reshape(block), out_a.reshape(block)
    sends = pack((grad_a, grad_b, out_a), (None, None, None), targets)
    out_b, sends = lax.optimization_barrier((out_b, sends))
    back = exchange(sends, size)
    out_b = spread(shuffle(out_b, source), groups).reshape(block)
    back, out_b = settle(back, out_b)
    late = exchange(pack((out_b,), (None,), targets), size)
    grads = unpack((grad_a, grad_b), back, ((0, 0), (0, 1)), origins)
    outputs = unpack((out_a, out_b), back + late, ((0, 2), (len(back), 0)), origins)
    return (outputs, grads)


def solution(mesh):
    spec = P("grp", None, "sp", None)
    return jax.shard_map(
        on_device, mesh=mesh, in_specs=(spec, P(), P(), P(), P(), spec), out_specs=(spec, spec), check_vma=False
    )
```

```python
import functools
import jax
import jax.numpy as jnp
from jax import lax
from jax.experimental import pallas as pl
from jax.experimental.pallas import tpu as pltpu
from jax.sharding import PartitionSpec as P

HEADS = 16
HP = 80
GROUPS = 4
EPS = 1e-06
F32 = jnp.float32
BF16 = jnp.bfloat16
LOG2E = 1.4426950408889634
MIB = 1024 * 1024
IN_VMEM = pl.BlockSpec(memory_space=pltpu.VMEM)
IN_SMEM = pl.BlockSpec(memory_space=pltpu.SMEM)
ANYWHERE = pl.BlockSpec(memory_space=pltpu.HBM)


def dot_nn(a, b):
    return lax.dot_general(a, b, (((1,), (0,)), ((), ())), preferred_element_type=F32)


def dot_nt(a, b):
    return lax.dot_general(a, b, (((1,), (1,)), ((), ())), preferred_element_type=F32)


def dot_tn(a, b):
    return lax.dot_general(a, b, (((0,), (0,)), ((), ())), preferred_element_type=F32)


def cost(flops, moved):
    return pl.CostEstimate(flops=flops, bytes_accessed=moved, transcendentals=0)


def far(x):
    return pltpu.with_memory_space_constraint(x, pltpu.HBM)


def copy_all(pairs, sems):
    return [pltpu.make_async_copy(src, dst, sems.at[n]) for n, (src, dst) in enumerate(pairs)]


def start_all(copies):
    for copy in copies:
        copy.start()


def wait_all(copies):
    for copy in copies:
        copy.wait()


def prepare_kernel(wq_hbm, wo_hbm, wt_hbm, wop_hbm, wt_ref, wop_ref, out_sems, wq, wo, sems):
    width = wo.shape[0]
    hd = width // HEADS
    loads = [
        pltpu.make_async_copy(wq_hbm.at[:, pl.ds(j * width, width)], wq.at[j], sems.at[j]) for j in range(3)
    ]
    loads.append(pltpu.make_async_copy(wo_hbm, wo, sems.at[3]))
    for load in loads:
        load.start()
    pad = jnp.zeros((HP - hd, width), F32)

    def put(dst, rows, j):
        for h in range(HEADS):
            part = jnp.concatenate([rows[h * hd:(h + 1) * hd], pad])
            dst[pl.ds((j * HEADS + h) * HP, HP), :] = part.astype(BF16)

    saves = []
    for j in range(3):
        loads[j].wait()
        put(wt_ref, wq[j].astype(F32).T, j)
        part = pl.ds(j * HEADS * HP, HEADS * HP)
        saves.append(pltpu.make_async_copy(wt_ref.at[part], wt_hbm.at[part], out_sems.at[j]))
        saves[-1].start()
    loads[3].wait()
    put(wop_ref, wo[...].astype(F32), 0)
    saves.append(pltpu.make_async_copy(wop_ref, wop_hbm, out_sems.at[3]))
    saves[-1].start()
    wait_all(saves)


def prepare(weight_qkv, weight_out):
    width = weight_out.shape[0]
    return pl.pallas_call(
        prepare_kernel,
        out_shape=(pltpu.HBM((3 * HEADS * HP, width), BF16), pltpu.HBM((HEADS * HP, width), BF16)),
        in_specs=[ANYWHERE] * 2,
        out_specs=(ANYWHERE, ANYWHERE),
        scratch_shapes=[
            pltpu.VMEM((3 * HEADS * HP, width), BF16),
            pltpu.VMEM((HEADS * HP, width), BF16),
            pltpu.SemaphoreType.DMA((4,)),
            pltpu.VMEM((3, width, width), BF16),
            pltpu.VMEM((width, width), BF16),
            pltpu.SemaphoreType.DMA((4,)),
        ],
        compiler_params=pltpu.CompilerParams(vmem_limit_bytes=40 * MIB),
        cost_estimate=cost(0, 0),
        name="prepare",
    )(far(weight_qkv), far(weight_out))


def regroup(x, outer, inner):
    rows = x.shape[0]
    to = lax.broadcasted_iota(jnp.int32, (rows, rows), 0)
    at = lax.broadcasted_iota(jnp.int32, (rows, rows), 1)
    wanted = to // 2 % outer * (2 * inner) + to // (2 * outer) * 2 + to % 2
    return dot_nn((at == wanted).astype(BF16), x).astype(BF16)


def group_rows():
    per = HEADS // GROUPS
    return [pl.ds((j * HEADS + g * per) * HP, HP * per) for g in range(GROUPS) for j in range(3)]


def assemble(dst, f, own, part_of, pieces, from_ref, sems):
    count = sems.shape[1]
    part = own.shape[1]
    copies = []
    for n in range(count):
        if pieces:
            at = from_ref[n]
            src = pieces[n - 1].at[part_of] if n else own.at[at]
        else:
            at = n
            src = own.at[n]
        copies.append(pltpu.make_async_copy(src, dst.at[pl.ds(f * count * part + at * part, part)], sems.at[f, n]))
    for copy in copies:
        copy.start()
    return copies


def forward_kernel(scale, from_ref, keep_ref, wt_hbm, wo_hbm, clips, *rest):
    pieces, (out_a, out_b, x_hbm, qkv_hbm, p_hbm, inverse) = rest[:-19], rest[-19:-13]
    nrm, att, sbuf, sems, x_ref, qkv, probs, wt, wo, total, wsem, osem, ssem = rest[-13:]
    copies = []
    for f in range(2):
        copies += assemble(x_ref, f, clips.at[f], f, pieces, from_ref, sems)
    parts = group_rows()
    weights = copy_all([(wt_hbm.at[part], wt.at[part]) for part in parts], wsem)
    out_weight = copy_all([(wo_hbm, wo)], osem)
    start_all(weights[:3])
    wait_all(copies)
    start_all(weights[3:6])
    toks = x_ref.shape[0]
    frames = toks // 256
    per = HEADS // GROUPS
    rows = HP * per
    third = HEADS * HP
    x = x_ref[...].astype(F32)
    mean = jnp.mean(x, axis=-1, keepdims=True)
    centered = x - mean
    var = jnp.mean(centered * centered, axis=-1, keepdims=True)
    nrm[...] = (centered * lax.rsqrt(var + EPS)).astype(BF16)
    units = [(h, f) for h in range(HEADS) for f in range(frames)]

    def project(g):
        for j in range(3):
            part = pl.ds(j * third + g * rows, rows)
            qkv[part, :] = dot_nt(wt[part, :], nrm[...]).astype(BF16)

    def scores(i):
        h, f = units[i]
        cols = pl.ds(f * 256, 256)
        q = qkv[pl.ds(HP * h, HP), cols]
        k = qkv[pl.ds(third + HP * h, HP), cols]
        sbuf[i % 2] = dot_tn(k, q)

    def soften(i):
        h, f = units[i]
        s = sbuf[i % 2]
        top = jnp.max(s, axis=0, keepdims=True)
        e = jnp.exp2((s - top) * (scale * LOG2E))
        probs[h, :, pl.ds(f * 256, 256)] = e.astype(BF16)
        inv = 1.0 / jnp.sum(e, axis=0, keepdims=True)
        inverse[h, :, pl.ds(f * 256, 256)] = inv

    def mix(i):
        h, f = units[i]
        cols = pl.ds(f * 256, 256)
        v = qkv[pl.ds(2 * third + HP * h, HP), cols]
        att[pl.ds(HP * h, HP), cols] = (dot_nn(v, probs[h, :, cols]) * inverse[h, :, cols]).astype(BF16)

    wait_all(weights[:3])
    start_all(weights[6:9])
    project(0)
    scores(0)
    for i in range(len(units)):
        h, f = units[i]
        if f == 0 and h % per == per - 2 and h // per + 1 < GROUPS:
            g = h // per + 1
            wait_all(weights[3 * g:3 * g + 3])
            if g == 1:
                start_all(weights[9:] + out_weight)
            project(g)
        if f == 0 and h == HEADS // 2 + 1:
            half = pl.ds(0, HEADS // 2)
            saves = [pltpu.make_async_copy(probs.at[half], p_hbm.at[half], ssem.at[0])]
            saves[-1].start()
        if f == 0 and h == HEADS - per:
            saves += [
                pltpu.make_async_copy(qkv, qkv_hbm, ssem.at[1]),
                pltpu.make_async_copy(x_ref, x_hbm, ssem.at[2]),
            ]
            saves[-1].start()
            saves[-2].start()
        if i + 1 < len(units):
            scores(i + 1)
        soften(i)
        if i:
            mix(i - 1)
    mix(len(units) - 1)
    half = pl.ds(HEADS // 2, HEADS // 2)
    saves.append(pltpu.make_async_copy(probs.at[half], p_hbm.at[half], ssem.at[3]))
    saves[-1].start()
    wait_all(out_weight)
    projected = dot_tn(att[...], wo[...])
    total[...] = (x_ref[...].astype(F32) + projected).astype(BF16)
    for f, out_ref in enumerate((out_a, out_b)):
        part = pl.ds(f * 256, 256)

        @pl.when(keep_ref[f] == 0)
        def _():
            total[part] = jnp.zeros((256, total.shape[1]), BF16)

        if f:
            total[part] = regroup(total[part], sems.shape[1], 256 // (2 * sems.shape[1]))
        saves.append(pltpu.make_async_copy(total.at[part], out_ref, ssem.at[4 + f]))
        saves[-1].start()
    wait_all(saves)


def forward(clips, pieces, origins, keep, wt, wo, scale):
    frames, part, width = clips.shape[1:]
    toks = frames * part
    out = pltpu.HBM((toks, width), BF16)
    return pl.pallas_call(
        functools.partial(forward_kernel, scale),
        out_shape=(
            out,
            out,
            pltpu.HBM((2 * toks, width), BF16),
            pltpu.HBM((wt.shape[0], 2 * toks), BF16),
            pltpu.HBM((HEADS, toks, 2 * toks), BF16),
            jax.ShapeDtypeStruct((HEADS, 1, 2 * toks), F32),
        ),
        in_specs=[IN_SMEM] * 2 + [ANYWHERE] * (3 + len(pieces)),
        out_specs=(ANYWHERE,) * 5 + (IN_VMEM,),
        scratch_shapes=[
            pltpu.VMEM((2 * toks, width), BF16),
            pltpu.VMEM((wo.shape[0], 2 * toks), BF16),
            pltpu.VMEM((2, toks, toks), F32),
            pltpu.SemaphoreType.DMA((2, frames)),
            pltpu.VMEM((2 * toks, width), BF16),
            pltpu.VMEM((wt.shape[0], 2 * toks), BF16),
            pltpu.VMEM((HEADS, toks, 2 * toks), BF16),
            pltpu.VMEM(wt.shape, BF16),
            pltpu.VMEM(wo.shape, BF16),
            pltpu.VMEM((2 * toks, width), BF16),
            pltpu.SemaphoreType.DMA((3 * GROUPS,)),
            pltpu.SemaphoreType.DMA((1,)),
            pltpu.SemaphoreType.DMA((6,)),
        ],
        compiler_params=pltpu.CompilerParams(vmem_limit_bytes=48 * MIB),
        cost_estimate=cost(4 * toks * (wt.size + wo.size) + 8 * wo.shape[0] * toks * toks, 2 * (wt.size + wo.size)),
        name="forward",
    )(origins, keep, far(wt), far(wo), far(clips), *[far(x) for x in pieces])


def backward_kernel(scale, from_ref, keep_ref, inverse, wt_hbm, wo_hbm, x_hbm, qkv_hbm, p_hbm, cot_a, cot_b, *rest):
    pieces, (ga_ref, gb_ref, c_ref, gatt, gqkv, gabuf, gpbuf, gsbuf, sems) = rest[:-19], rest[-19:-10]
    x_ref, qkv, probs, wt, wo, total, lsem, gsem, tsem, ssem = rest[-10:]
    copies = assemble(c_ref, 0, cot_a, 2, pieces, from_ref, sems) + assemble(c_ref, 1, cot_b, 0, [], from_ref, sems)
    per = HEADS // GROUPS
    parts = group_rows()
    heads = [pl.ds(g * per, per) for g in range(GROUPS)]
    quarter = wt.shape[0] // GROUPS
    rows = [pl.ds(g * quarter, quarter) for g in range(GROUPS)]
    load_wo = copy_all([(wo_hbm, wo)], lsem)
    loads = [
        copy_all([(qkv_hbm.at[part], qkv.at[part]) for part in parts[3 * g:3 * g + 3]]
                 + [(p_hbm.at[heads[g]], probs.at[heads[g]])], gsem.at[g])
        for g in range(GROUPS)
    ]
    late = copy_all([(wt_hbm.at[part], wt.at[part]) for part in rows] + [(x_hbm, x_ref)], tsem)
    start_all(load_wo)
    wait_all(copies)
    start_all(loads[0])
    for f in range(2):
        part = c_ref[pl.ds(f * 256, 256)]
        c_ref[pl.ds(f * 256, 256)] = jnp.where(keep_ref[f] > 0, part, jnp.zeros_like(part))
    toks = x_ref.shape[0]
    frames = toks // 256
    third = HEADS * HP
    wait_all(load_wo)
    start_all(loads[1])
    gatt[...] = dot_nt(wo[...], c_ref[...])
    wait_all(loads[0])
    start_all(late[:1])
    units = [(h, f) for h in range(HEADS) for f in range(frames)]

    def rows_of(h):
        return [pl.ds(j * third + HP * h, HP) for j in range(3)]

    def reach(i):
        h, f = units[i]
        cols = pl.ds(f * 256, 256)
        part = pl.ds(HP * h, HP)
        ga = (gatt[part, cols] * inverse[h, :, cols]).astype(BF16)
        gabuf[i % 2] = ga
        gpbuf[i % 2] = dot_tn(qkv[rows_of(h)[2], cols], ga)

    def soften(i):
        h, f = units[i]
        cols = pl.ds(f * 256, 256)
        gp = gpbuf[i % 2]
        e = probs[h, :, cols].astype(F32)
        mass = jnp.sum(e * gp, axis=0, keepdims=True) * inverse[h, :, cols]
        gsbuf[i % 2] = (e * (gp - mass) * scale).astype(BF16)

    def spread(i):
        h, f = units[i]
        cols = pl.ds(f * 256, 256)
        at = rows_of(h)
        gs = gsbuf[i % 2]
        gqkv[at[0], cols] = dot_nn(qkv[at[1], cols], gs).astype(BF16)
        gqkv[at[1], cols] = dot_nt(qkv[at[0], cols], gs).astype(BF16)

    def values(i):
        h, f = units[i]
        cols = pl.ds(f * 256, 256)
        gqkv[rows_of(h)[2], cols] = dot_nt(gabuf[i % 2], probs[h, :, cols]).astype(BF16)

    reach(0)
    for i in range(len(units)):
        values(i)
        if i + 1 < len(units):
            h, f = units[i + 1]
            if f == 0 and h % per == 0:
                g = h // per
                wait_all(loads[g])
                start_all(late[g:g + 1])
                start_all(loads[g + 1] if g + 1 < GROUPS else late[GROUPS:])
            reach(i + 1)
        soften(i)
        if i:
            spread(i - 1)
    spread(len(units) - 1)
    wait_all(late)
    gn = dot_tn(gqkv[...], wt[...])
    x = x_ref[...].astype(F32)
    mean = jnp.mean(x, axis=-1, keepdims=True)
    centered = x - mean
    var = jnp.mean(centered * centered, axis=-1, keepdims=True)
    inv = lax.rsqrt(var + EPS)
    n = centered * inv
    gx = inv * (gn - jnp.mean(gn, axis=-1, keepdims=True) - n * jnp.mean(gn * n, axis=-1, keepdims=True))
    total[...] = (c_ref[...].astype(F32) + gx).astype(BF16)
    saves = copy_all([(total.at[pl.ds(0, 256)], ga_ref), (total.at[pl.ds(256, 256)], gb_ref)], ssem)
    start_all(saves)
    wait_all(saves)


def backward(cot_a, cot_b, pieces, origins, keep, wt, wo, kept, scale):
    frames, part, width = cot_a.shape
    toks = frames * part
    x, qkv, probs, inverse = kept
    out = pltpu.HBM((toks, width), BF16)
    return pl.pallas_call(
        functools.partial(backward_kernel, scale),
        out_shape=(out, out),
        in_specs=[IN_SMEM] * 2 + [IN_VMEM] + [ANYWHERE] * (7 + len(pieces)),
        out_specs=(ANYWHERE, ANYWHERE),
        scratch_shapes=[
            pltpu.VMEM((2 * toks, width), BF16),
            pltpu.VMEM((wo.shape[0], 2 * toks), F32),
            pltpu.VMEM(qkv.shape, BF16),
            pltpu.VMEM((2, HP, toks), BF16),
            pltpu.VMEM((2, toks, toks), F32),
            pltpu.VMEM((2, toks, toks), BF16),
            pltpu.SemaphoreType.DMA((2, frames)),
            pltpu.VMEM(x.shape, BF16),
            pltpu.VMEM(qkv.shape, BF16),
            pltpu.VMEM(probs.shape, BF16),
            pltpu.VMEM(wt.shape, BF16),
            pltpu.VMEM(wo.shape, BF16),
            pltpu.VMEM(x.shape, BF16),
            pltpu.SemaphoreType.DMA((1,)),
            pltpu.SemaphoreType.DMA((GROUPS, 4)),
            pltpu.SemaphoreType.DMA((GROUPS + 1,)),
            pltpu.SemaphoreType.DMA((2,)),
        ],
        compiler_params=pltpu.CompilerParams(vmem_limit_bytes=48 * MIB),
        cost_estimate=cost(4 * toks * (wt.size + wo.size) + 16 * wo.shape[0] * toks * toks, 2 * (wt.size + wo.size)),
        name="backward",
    )(origins, keep, inverse, *[far(x) for x in (wt, wo, x, qkv, probs, cot_a, cot_b)], *[far(x) for x in pieces])


def shuffle_kernel(index_ref, x_ref, out_ref):
    for i in range(x_ref.shape[0]):
        out_ref[i] = x_ref[index_ref[i]]


def shuffle(x, index):
    return pl.pallas_call(
        shuffle_kernel,
        out_shape=jax.ShapeDtypeStruct(x.shape, x.dtype),
        in_specs=[IN_SMEM, IN_VMEM],
        out_specs=IN_VMEM,
        compiler_params=pltpu.CompilerParams(vmem_limit_bytes=8 * MIB),
        name="shuffle",
    )(index, x)


def spread(x, groups):
    return lax.all_to_all(x.reshape(groups, -1, x.shape[-1]), "grp", 0, 0, tiled=True)


def pack_kernel(leads, whole, to_ref, *refs):
    count = len(leads)
    sources, outs, sems = refs[:count], refs[count:-1], refs[-1]
    copies = []
    if whole is not None:
        copies.append(pltpu.make_async_copy(sources[-1].at[whole], outs[-1], sems.at[len(outs) - 1, 0]))
        outs = outs[:-1]
    for n, out in enumerate(outs):
        at = to_ref[n + 1]
        for a, lead in enumerate(leads):
            src = sources[a] if lead is None else sources[a].at[lead[0]]
            copies.append(pltpu.make_async_copy(src.at[at], out.at[a], sems.at[n, a]))
    for copy in copies:
        copy.start()
    for copy in copies:
        copy.wait()


def pack(sources, leads, targets, whole=None):
    n = targets.shape[0]
    block = sources[0].shape[-2:]
    shapes = (jax.ShapeDtypeStruct((len(leads),) + block, BF16),) * (n - 1)
    if whole is not None:
        shapes += (jax.ShapeDtypeStruct(sources[-1].shape[1:], BF16),)
    return pl.pallas_call(
        functools.partial(pack_kernel, leads, whole),
        out_shape=shapes,
        in_specs=[IN_SMEM] + [ANYWHERE] * len(sources),
        out_specs=(IN_VMEM,) * len(shapes),
        scratch_shapes=[pltpu.SemaphoreType.DMA((len(shapes), len(leads)))],
        compiler_params=pltpu.CompilerParams(vmem_limit_bytes=12 * MIB),
        name="pack",
    )(targets, *[far(x) for x in sources])


def unpack_kernel(picks, from_ref, *refs):
    owns = len(picks)
    sources, (*outs, held, in_sems, out_sems) = refs[:-5], refs[-5:]
    own, pieces = sources[:owns], sources[owns:]
    frames = in_sems.shape[1]
    reads, writes = [], []
    for a, pick in enumerate(picks):
        for n in range(frames):
            if pick is None:
                at, src = n, own[a].at[n]
            else:
                at = from_ref[n]
                src = pieces[n - 1].at[pick] if n else own[a].at[at]
            reads.append(pltpu.make_async_copy(src, held.at[a, n], in_sems.at[a, n]))
            writes.append(pltpu.make_async_copy(held.at[a, n], outs[a // 2].at[a % 2, at], out_sems.at[a, n]))
    start_all(reads)
    for a, pick in enumerate(picks):
        mine = slice(a * frames, (a + 1) * frames)
        wait_all(reads[mine])
        if pick is None:
            rows = held[a].reshape(-1, held.shape[-1])
            held[a] = regroup(rows, rows.shape[0] // (2 * frames), frames).reshape(held.shape[1:])
        start_all(writes[mine])
    wait_all(writes)


def unpack(own, pieces, picks, origins):
    n = origins.shape[0]
    shape = own[0].shape
    return pl.pallas_call(
        functools.partial(unpack_kernel, picks),
        out_shape=(pltpu.HBM((2,) + shape, BF16),) * 2,
        in_specs=[IN_SMEM] + [ANYWHERE] * (len(own) + len(pieces)),
        out_specs=(ANYWHERE,) * 2,
        scratch_shapes=[
            pltpu.VMEM((len(picks),) + shape, BF16),
            pltpu.SemaphoreType.DMA((len(picks), n)),
            pltpu.SemaphoreType.DMA((len(picks), n)),
        ],
        compiler_params=pltpu.CompilerParams(vmem_limit_bytes=12 * MIB),
        name="unpack",
    )(origins, *[far(x) for x in own], *[far(x) for x in pieces])


def exchange(sends, size):
    chips = size // 2
    out = []
    for n, x in enumerate(sends, start=1):
        pairs = [(i, (i // 2 + n // 2) % chips * 2 + (i % 2 ^ n % 2)) for i in range(size)]
        out.append(lax.ppermute(x, "sp", pairs))
    return out


def on_device(clips, counts, dest, weight_qkv, weight_out, cotangent):
    groups = lax.axis_size("grp")
    size = lax.axis_size("sp")
    me = lax.axis_index("grp")
    frame = lax.axis_index("sp")
    order = jnp.arange(groups, dtype=jnp.int32)
    source = jnp.sum(jnp.where(dest[None, :] == order[:, None], order[None, :], 0), axis=1)
    offset = jnp.arange(size, dtype=jnp.int32)
    targets = (frame // 2 + offset // 2) % (size // 2) * 2 + (frame + offset) % 2
    origins = (frame // 2 - offset // 2) % (size // 2) * 2 + (frame + offset) % 2
    scale = (weight_out.shape[0] // HEADS) ** -0.5
    used = lax.dynamic_slice_in_dim(counts, 2 * me, 2)
    keep = (frame < used).astype(jnp.int32)
    keep_a, keep_b = keep[0:1], keep[1:2]

    block = clips.shape[1:]
    width = block[-1]
    *sends, cot_b = pack((clips, clips, cotangent), ((0,), (1,), (0,)), targets, whole=1)
    cot_b = spread(cot_b, groups)
    pieces = exchange(sends, size)
    cot_b = shuffle(cot_b, dest)
    weight_qkv, cot_b = lax.optimization_barrier((weight_qkv, cot_b))
    wt, wo = prepare(weight_qkv, weight_out)
    cot_b = spread(cot_b, groups).reshape(block)
    cot_b, wt = lax.optimization_barrier((cot_b, wt))
    out_a, out_b, *kept = forward(clips, pieces, origins, keep, wt, wo, scale)
    cot_b = lax.all_to_all(cot_b, "sp", 0, 0, tiled=True)
    cot_b, out_b = lax.optimization_barrier((cot_b, out_b))
    out_b = spread(out_b, groups)
    grad_a, grad_b = backward(cotangent[0], cot_b, pieces, origins, keep, wt, wo, kept, scale)
    grad_a, grad_b, out_a = grad_a.reshape(block), grad_b.reshape(block), out_a.reshape(block)
    out_b, grad_a = lax.optimization_barrier((out_b, grad_a))
    out_b = shuffle(out_b, source).reshape(groups * size, -1, width)
    out_b = lax.all_to_all(out_b, ("grp", "sp"), 0, 0, tiled=True).reshape(block)
    back = exchange(pack((grad_a, grad_b, out_a), (None, None, None), targets), size)
    grads, outputs = unpack((grad_a, grad_b, out_a, out_b), back, (0, 1, 2, None), origins)
    return (outputs, grads)


def solution(mesh):
    spec = P("grp", None, "sp", None)
    return jax.shard_map(
        on_device, mesh=mesh, in_specs=(spec, P(), P(), P(), P(), spec), out_specs=(spec, spec), check_vma=False
    )
```

```python
import functools
import jax
import jax.numpy as jnp
from jax import lax
from jax.experimental import pallas as pl
from jax.experimental.pallas import tpu as pltpu
from jax.sharding import PartitionSpec as P

HEADS = 16
HP = 80
GROUPS = 4
EPS = 1e-06
F32 = jnp.float32
BF16 = jnp.bfloat16
LOG2E = 1.4426950408889634
MIB = 1024 * 1024
IN_VMEM = pl.BlockSpec(memory_space=pltpu.VMEM)
IN_SMEM = pl.BlockSpec(memory_space=pltpu.SMEM)
ANYWHERE = pl.BlockSpec(memory_space=pltpu.HBM)


def dot_nn(a, b):
    return lax.dot_general(a, b, (((1,), (0,)), ((), ())), preferred_element_type=F32)


def dot_nt(a, b):
    return lax.dot_general(a, b, (((1,), (1,)), ((), ())), preferred_element_type=F32)


def dot_tn(a, b):
    return lax.dot_general(a, b, (((0,), (0,)), ((), ())), preferred_element_type=F32)


def cost(flops, moved):
    return pl.CostEstimate(flops=flops, bytes_accessed=moved, transcendentals=0)


def far(x):
    return pltpu.with_memory_space_constraint(x, pltpu.HBM)


def copy_all(pairs, sems):
    return [pltpu.make_async_copy(src, dst, sems.at[n]) for n, (src, dst) in enumerate(pairs)]


def start_all(copies):
    for copy in copies:
        copy.start()


def wait_all(copies):
    for copy in copies:
        copy.wait()


def prepare_kernel(wq_hbm, wo_hbm, wt_hbm, wop_hbm, wt_ref, wop_ref, out_sems, wq, wo, sems):
    width = wo.shape[0]
    hd = width // HEADS
    loads = [
        pltpu.make_async_copy(wq_hbm.at[:, pl.ds(j * width, width)], wq.at[j], sems.at[j]) for j in range(3)
    ]
    loads.append(pltpu.make_async_copy(wo_hbm, wo, sems.at[3]))
    for load in loads:
        load.start()
    pad = jnp.zeros((HP - hd, width), F32)

    def put(dst, rows, j):
        for h in range(HEADS):
            part = jnp.concatenate([rows[h * hd:(h + 1) * hd], pad])
            dst[pl.ds((j * HEADS + h) * HP, HP), :] = part.astype(BF16)

    saves = []
    for j in range(3):
        loads[j].wait()
        put(wt_ref, wq[j].astype(F32).T, j)
        part = pl.ds(j * HEADS * HP, HEADS * HP)
        saves.append(pltpu.make_async_copy(wt_ref.at[part], wt_hbm.at[part], out_sems.at[j]))
        saves[-1].start()
    loads[3].wait()
    put(wop_ref, wo[...].astype(F32), 0)
    saves.append(pltpu.make_async_copy(wop_ref, wop_hbm, out_sems.at[3]))
    saves[-1].start()
    wait_all(saves)


def prepare(weight_qkv, weight_out):
    width = weight_out.shape[0]
    return pl.pallas_call(
        prepare_kernel,
        out_shape=(pltpu.HBM((3 * HEADS * HP, width), BF16), pltpu.HBM((HEADS * HP, width), BF16)),
        in_specs=[ANYWHERE] * 2,
        out_specs=(ANYWHERE, ANYWHERE),
        scratch_shapes=[
            pltpu.VMEM((3 * HEADS * HP, width), BF16),
            pltpu.VMEM((HEADS * HP, width), BF16),
            pltpu.SemaphoreType.DMA((4,)),
            pltpu.VMEM((3, width, width), BF16),
            pltpu.VMEM((width, width), BF16),
            pltpu.SemaphoreType.DMA((4,)),
        ],
        compiler_params=pltpu.CompilerParams(vmem_limit_bytes=40 * MIB),
        cost_estimate=cost(0, 0),
        name="prepare",
    )(far(weight_qkv), far(weight_out))


def regroup(x, outer, inner):
    rows = x.shape[0]
    to = lax.broadcasted_iota(jnp.int32, (rows, rows), 0)
    at = lax.broadcasted_iota(jnp.int32, (rows, rows), 1)
    wanted = to // 2 % outer * (2 * inner) + to // (2 * outer) * 2 + to % 2
    return dot_nn((at == wanted).astype(BF16), x).astype(BF16)


def group_rows():
    per = HEADS // GROUPS
    return [pl.ds((j * HEADS + g * per) * HP, HP * per) for g in range(GROUPS) for j in range(3)]


def assemble(dst, f, own, part_of, pieces, from_ref, sems):
    count = sems.shape[1]
    part = own.shape[1]
    copies = []
    for n in range(count):
        if pieces:
            at = from_ref[n]
            src = pieces[n - 1].at[part_of] if n else own.at[at]
        else:
            at = n
            src = own.at[n]
        copies.append(pltpu.make_async_copy(src, dst.at[pl.ds(f * count * part + at * part, part)], sems.at[f, n]))
    for copy in copies:
        copy.start()
    return copies


def forward_kernel(scale, from_ref, keep_ref, wt_hbm, wo_hbm, clips, *rest):
    pieces, (out_a, out_b, x_hbm, qkv_hbm, p_hbm, inverse) = rest[:-19], rest[-19:-13]
    nrm, att, sbuf, sems, x_ref, qkv, probs, wt, wo, total, wsem, osem, ssem = rest[-13:]
    copies = []
    for f in range(2):
        copies += assemble(x_ref, f, clips.at[f], f, pieces, from_ref, sems)
    parts = group_rows()
    weights = copy_all([(wt_hbm.at[part], wt.at[part]) for part in parts], wsem)
    out_weight = copy_all([(wo_hbm, wo)], osem)
    start_all(weights[:6])
    wait_all(copies)
    toks = x_ref.shape[0]
    frames = toks // 256
    per = HEADS // GROUPS
    rows = HP * per
    third = HEADS * HP
    x = x_ref[...].astype(F32)
    mean = jnp.mean(x, axis=-1, keepdims=True)
    centered = x - mean
    var = jnp.mean(centered * centered, axis=-1, keepdims=True)
    nrm[...] = (centered * lax.rsqrt(var + EPS)).astype(BF16)
    units = [(h, f) for h in range(HEADS) for f in range(frames)]

    def project(g):
        for j in range(3):
            part = pl.ds(j * third + g * rows, rows)
            qkv[part, :] = dot_nt(wt[part, :], nrm[...]).astype(BF16)

    def scores(i):
        h, f = units[i]
        cols = pl.ds(f * 256, 256)
        q = qkv[pl.ds(HP * h, HP), cols]
        k = qkv[pl.ds(third + HP * h, HP), cols]
        sbuf[i % 2] = dot_tn(k, q)

    def soften(i):
        h, f = units[i]
        s = sbuf[i % 2]
        top = jnp.max(s, axis=0, keepdims=True)
        e = jnp.exp2((s - top) * (scale * LOG2E))
        probs[h, :, pl.ds(f * 256, 256)] = e.astype(BF16)
        inv = 1.0 / jnp.sum(e, axis=0, keepdims=True)
        inverse[h, :, pl.ds(f * 256, 256)] = inv

    def mix(i):
        h, f = units[i]
        cols = pl.ds(f * 256, 256)
        v = qkv[pl.ds(2 * third + HP * h, HP), cols]
        att[pl.ds(HP * h, HP), cols] = (dot_nn(v, probs[h, :, cols]) * inverse[h, :, cols]).astype(BF16)

    wait_all(weights[:3])
    start_all(weights[6:9])
    project(0)
    scores(0)
    for i in range(len(units)):
        h, f = units[i]
        if f == 0 and h % per == per - 2 and h // per + 1 < GROUPS:
            g = h // per + 1
            wait_all(weights[3 * g:3 * g + 3])
            if g == 1:
                start_all(weights[9:] + out_weight)
            project(g)
        if f == 0 and h == HEADS // 2 + 1:
            half = pl.ds(0, HEADS // 2)
            saves = [pltpu.make_async_copy(probs.at[half], p_hbm.at[half], ssem.at[0])]
            saves[-1].start()
        if f == 0 and h == HEADS - per:
            saves += [
                pltpu.make_async_copy(qkv, qkv_hbm, ssem.at[1]),
                pltpu.make_async_copy(x_ref, x_hbm, ssem.at[2]),
            ]
            saves[-1].start()
            saves[-2].start()
        if i + 1 < len(units):
            scores(i + 1)
        soften(i)
        if i:
            mix(i - 1)
    mix(len(units) - 1)
    half = pl.ds(HEADS // 2, HEADS // 2)
    saves.append(pltpu.make_async_copy(probs.at[half], p_hbm.at[half], ssem.at[3]))
    saves[-1].start()
    wait_all(out_weight)
    projected = dot_tn(att[...], wo[...])
    total[...] = (x_ref[...].astype(F32) + projected).astype(BF16)
    for f, out_ref in enumerate((out_a, out_b)):
        part = pl.ds(f * 256, 256)

        @pl.when(keep_ref[f] == 0)
        def _():
            total[part] = jnp.zeros((256, total.shape[1]), BF16)

        if f:
            total[part] = regroup(total[part], sems.shape[1], 256 // (2 * sems.shape[1]))
        saves.append(pltpu.make_async_copy(total.at[part], out_ref, ssem.at[4 + f]))
        saves[-1].start()
    wait_all(saves)


def forward(clips, pieces, origins, keep, wt, wo, scale):
    frames, part, width = clips.shape[1:]
    toks = frames * part
    out = pltpu.HBM((toks, width), BF16)
    return pl.pallas_call(
        functools.partial(forward_kernel, scale),
        out_shape=(
            out,
            out,
            pltpu.HBM((2 * toks, width), BF16),
            pltpu.HBM((wt.shape[0], 2 * toks), BF16),
            pltpu.HBM((HEADS, toks, 2 * toks), BF16),
            jax.ShapeDtypeStruct((HEADS, 1, 2 * toks), F32),
        ),
        in_specs=[IN_SMEM] * 2 + [ANYWHERE] * (3 + len(pieces)),
        out_specs=(ANYWHERE,) * 5 + (IN_VMEM,),
        scratch_shapes=[
            pltpu.VMEM((2 * toks, width), BF16),
            pltpu.VMEM((wo.shape[0], 2 * toks), BF16),
            pltpu.VMEM((2, toks, toks), F32),
            pltpu.SemaphoreType.DMA((2, frames)),
            pltpu.VMEM((2 * toks, width), BF16),
            pltpu.VMEM((wt.shape[0], 2 * toks), BF16),
            pltpu.VMEM((HEADS, toks, 2 * toks), BF16),
            pltpu.VMEM(wt.shape, BF16),
            pltpu.VMEM(wo.shape, BF16),
            pltpu.VMEM((2 * toks, width), BF16),
            pltpu.SemaphoreType.DMA((3 * GROUPS,)),
            pltpu.SemaphoreType.DMA((1,)),
            pltpu.SemaphoreType.DMA((6,)),
        ],
        compiler_params=pltpu.CompilerParams(vmem_limit_bytes=48 * MIB),
        cost_estimate=cost(4 * toks * (wt.size + wo.size) + 8 * wo.shape[0] * toks * toks, 2 * (wt.size + wo.size)),
        name="forward",
    )(origins, keep, far(wt), far(wo), far(clips), *[far(x) for x in pieces])


def backward_kernel(scale, from_ref, keep_ref, inverse, wt_hbm, wo_hbm, x_hbm, qkv_hbm, p_hbm, cot_a, cot_b, *rest):
    pieces, (ga_ref, gb_ref, c_ref, gatt, gqkv, gabuf, gpbuf, gsbuf, sems) = rest[:-19], rest[-19:-10]
    x_ref, qkv, probs, wt, wo, total, lsem, gsem, tsem, ssem = rest[-10:]
    copies = assemble(c_ref, 0, cot_a, 2, pieces, from_ref, sems) + assemble(c_ref, 1, cot_b, 0, [], from_ref, sems)
    per = HEADS // GROUPS
    parts = group_rows()
    heads = [pl.ds(g * per, per) for g in range(GROUPS)]
    quarter = wt.shape[0] // GROUPS
    rows = [pl.ds(g * quarter, quarter) for g in range(GROUPS)]
    load_wo = copy_all([(wo_hbm, wo)], lsem)
    loads = [
        copy_all([(qkv_hbm.at[part], qkv.at[part]) for part in parts[3 * g:3 * g + 3]]
                 + [(p_hbm.at[heads[g]], probs.at[heads[g]])], gsem.at[g])
        for g in range(GROUPS)
    ]
    late = copy_all([(wt_hbm.at[part], wt.at[part]) for part in rows] + [(x_hbm, x_ref)], tsem)
    start_all(load_wo + loads[0])
    wait_all(copies)
    for f in range(2):
        part = c_ref[pl.ds(f * 256, 256)]
        c_ref[pl.ds(f * 256, 256)] = jnp.where(keep_ref[f] > 0, part, jnp.zeros_like(part))
    toks = x_ref.shape[0]
    frames = toks // 256
    third = HEADS * HP
    wait_all(load_wo)
    start_all(loads[1])
    gatt[...] = dot_nt(wo[...], c_ref[...])
    wait_all(loads[0])
    start_all(late[:1])
    units = [(h, f) for h in range(HEADS) for f in range(frames)]

    def rows_of(h):
        return [pl.ds(j * third + HP * h, HP) for j in range(3)]

    def reach(i):
        h, f = units[i]
        cols = pl.ds(f * 256, 256)
        part = pl.ds(HP * h, HP)
        ga = (gatt[part, cols] * inverse[h, :, cols]).astype(BF16)
        gabuf[i % 2] = ga
        gpbuf[i % 2] = dot_tn(qkv[rows_of(h)[2], cols], ga)

    def soften(i):
        h, f = units[i]
        cols = pl.ds(f * 256, 256)
        gp = gpbuf[i % 2]
        e = probs[h, :, cols].astype(F32)
        mass = jnp.sum(e * gp, axis=0, keepdims=True) * inverse[h, :, cols]
        gsbuf[i % 2] = (e * (gp - mass) * scale).astype(BF16)

    def spread(i):
        h, f = units[i]
        cols = pl.ds(f * 256, 256)
        at = rows_of(h)
        gs = gsbuf[i % 2]
        gqkv[at[0], cols] = dot_nn(qkv[at[1], cols], gs).astype(BF16)
        gqkv[at[1], cols] = dot_nt(qkv[at[0], cols], gs).astype(BF16)

    def values(i):
        h, f = units[i]
        cols = pl.ds(f * 256, 256)
        gqkv[rows_of(h)[2], cols] = dot_nt(gabuf[i % 2], probs[h, :, cols]).astype(BF16)

    reach(0)
    for i in range(len(units)):
        values(i)
        if i + 1 < len(units):
            h, f = units[i + 1]
            if f == 0 and h % per == 0:
                g = h // per
                wait_all(loads[g])
                start_all(late[g:g + 1])
                start_all(loads[g + 1] if g + 1 < GROUPS else late[GROUPS:])
            reach(i + 1)
        soften(i)
        if i:
            spread(i - 1)
    spread(len(units) - 1)
    wait_all(late)
    gn = dot_tn(gqkv[...], wt[...])
    x = x_ref[...].astype(F32)
    mean = jnp.mean(x, axis=-1, keepdims=True)
    centered = x - mean
    var = jnp.mean(centered * centered, axis=-1, keepdims=True)
    inv = lax.rsqrt(var + EPS)
    n = centered * inv
    gx = inv * (gn - jnp.mean(gn, axis=-1, keepdims=True) - n * jnp.mean(gn * n, axis=-1, keepdims=True))
    total[...] = (c_ref[...].astype(F32) + gx).astype(BF16)
    saves = copy_all([(total.at[pl.ds(0, 256)], ga_ref), (total.at[pl.ds(256, 256)], gb_ref)], ssem)
    start_all(saves)
    wait_all(saves)


def backward(cot_a, cot_b, pieces, origins, keep, wt, wo, kept, scale):
    frames, part, width = cot_a.shape
    toks = frames * part
    x, qkv, probs, inverse = kept
    out = pltpu.HBM((toks, width), BF16)
    return pl.pallas_call(
        functools.partial(backward_kernel, scale),
        out_shape=(out, out),
        in_specs=[IN_SMEM] * 2 + [IN_VMEM] + [ANYWHERE] * (7 + len(pieces)),
        out_specs=(ANYWHERE, ANYWHERE),
        scratch_shapes=[
            pltpu.VMEM((2 * toks, width), BF16),
            pltpu.VMEM((wo.shape[0], 2 * toks), F32),
            pltpu.VMEM(qkv.shape, BF16),
            pltpu.VMEM((2, HP, toks), BF16),
            pltpu.VMEM((2, toks, toks), F32),
            pltpu.VMEM((2, toks, toks), BF16),
            pltpu.SemaphoreType.DMA((2, frames)),
            pltpu.VMEM(x.shape, BF16),
            pltpu.VMEM(qkv.shape, BF16),
            pltpu.VMEM(probs.shape, BF16),
            pltpu.VMEM(wt.shape, BF16),
            pltpu.VMEM(wo.shape, BF16),
            pltpu.VMEM(x.shape, BF16),
            pltpu.SemaphoreType.DMA((1,)),
            pltpu.SemaphoreType.DMA((GROUPS, 4)),
            pltpu.SemaphoreType.DMA((GROUPS + 1,)),
            pltpu.SemaphoreType.DMA((2,)),
        ],
        compiler_params=pltpu.CompilerParams(vmem_limit_bytes=48 * MIB),
        cost_estimate=cost(4 * toks * (wt.size + wo.size) + 16 * wo.shape[0] * toks * toks, 2 * (wt.size + wo.size)),
        name="backward",
    )(origins, keep, inverse, *[far(x) for x in (wt, wo, x, qkv, probs, cot_a, cot_b)], *[far(x) for x in pieces])


def shuffle_kernel(index_ref, x_ref, out_ref):
    for i in range(x_ref.shape[0]):
        out_ref[i] = x_ref[index_ref[i]]


def shuffle(x, index):
    return pl.pallas_call(
        shuffle_kernel,
        out_shape=jax.ShapeDtypeStruct(x.shape, x.dtype),
        in_specs=[IN_SMEM, IN_VMEM],
        out_specs=IN_VMEM,
        compiler_params=pltpu.CompilerParams(vmem_limit_bytes=8 * MIB),
        name="shuffle",
    )(index, x)


def spread(x, groups):
    return lax.all_to_all(x.reshape(groups, -1, x.shape[-1]), "grp", 0, 0, tiled=True)


def pack_kernel(leads, whole, to_ref, *refs):
    count = len(leads)
    sources, outs, sems = refs[:count], refs[count:-1], refs[-1]
    copies = []
    if whole is not None:
        copies.append(pltpu.make_async_copy(sources[-1].at[whole], outs[-1], sems.at[len(outs) - 1, 0]))
        outs = outs[:-1]
    for n, out in enumerate(outs):
        at = to_ref[n + 1]
        for a, lead in enumerate(leads):
            src = sources[a] if lead is None else sources[a].at[lead[0]]
            copies.append(pltpu.make_async_copy(src.at[at], out.at[a], sems.at[n, a]))
    for copy in copies:
        copy.start()
    for copy in copies:
        copy.wait()


def pack(sources, leads, targets, whole=None):
    n = targets.shape[0]
    block = sources[0].shape[-2:]
    shapes = (jax.ShapeDtypeStruct((len(leads),) + block, BF16),) * (n - 1)
    if whole is not None:
        shapes += (jax.ShapeDtypeStruct(sources[-1].shape[1:], BF16),)
    return pl.pallas_call(
        functools.partial(pack_kernel, leads, whole),
        out_shape=shapes,
        in_specs=[IN_SMEM] + [ANYWHERE] * len(sources),
        out_specs=(IN_VMEM,) * len(shapes),
        scratch_shapes=[pltpu.SemaphoreType.DMA((len(shapes), len(leads)))],
        compiler_params=pltpu.CompilerParams(vmem_limit_bytes=12 * MIB),
        name="pack",
    )(targets, *[far(x) for x in sources])


def unpack_kernel(picks, from_ref, *refs):
    owns = len(picks)
    sources, (*outs, held, in_sems, out_sems) = refs[:-5], refs[-5:]
    own, pieces = sources[:owns], sources[owns:]
    frames = in_sems.shape[1]
    reads, writes = [], []
    for a, pick in enumerate(picks):
        for n in range(frames):
            if pick is None:
                at, src = n, own[a].at[n]
            else:
                at = from_ref[n]
                src = pieces[n - 1].at[pick] if n else own[a].at[at]
            reads.append(pltpu.make_async_copy(src, held.at[a, n], in_sems.at[a, n]))
            writes.append(pltpu.make_async_copy(held.at[a, n], outs[a // 2].at[a % 2, at], out_sems.at[a, n]))
    start_all(reads)
    for a, pick in enumerate(picks):
        mine = slice(a * frames, (a + 1) * frames)
        wait_all(reads[mine])
        if pick is None:
            rows = held[a].reshape(-1, held.shape[-1])
            held[a] = regroup(rows, rows.shape[0] // (2 * frames), frames).reshape(held.shape[1:])
        start_all(writes[mine])
    wait_all(writes)


def unpack(own, pieces, picks, origins):
    n = origins.shape[0]
    shape = own[0].shape
    return pl.pallas_call(
        functools.partial(unpack_kernel, picks),
        out_shape=(pltpu.HBM((2,) + shape, BF16),) * 2,
        in_specs=[IN_SMEM] + [ANYWHERE] * (len(own) + len(pieces)),
        out_specs=(ANYWHERE,) * 2,
        scratch_shapes=[
            pltpu.VMEM((len(picks),) + shape, BF16),
            pltpu.SemaphoreType.DMA((len(picks), n)),
            pltpu.SemaphoreType.DMA((len(picks), n)),
        ],
        compiler_params=pltpu.CompilerParams(vmem_limit_bytes=12 * MIB),
        name="unpack",
    )(origins, *[far(x) for x in own], *[far(x) for x in pieces])


def exchange(sends, size):
    chips = size // 2
    out = []
    for n, x in enumerate(sends, start=1):
        pairs = [(i, (i // 2 + n // 2) % chips * 2 + (i % 2 ^ n % 2)) for i in range(size)]
        out.append(lax.ppermute(x, "sp", pairs))
    return out


def on_device(clips, counts, dest, weight_qkv, weight_out, cotangent):
    groups = lax.axis_size("grp")
    size = lax.axis_size("sp")
    me = lax.axis_index("grp")
    frame = lax.axis_index("sp")
    order = jnp.arange(groups, dtype=jnp.int32)
    source = jnp.sum(jnp.where(dest[None, :] == order[:, None], order[None, :], 0), axis=1)
    offset = jnp.arange(size, dtype=jnp.int32)
    targets = (frame // 2 + offset // 2) % (size // 2) * 2 + (frame + offset) % 2
    origins = (frame // 2 - offset // 2) % (size // 2) * 2 + (frame + offset) % 2
    scale = (weight_out.shape[0] // HEADS) ** -0.5
    used = lax.dynamic_slice_in_dim(counts, 2 * me, 2)
    keep = (frame < used).astype(jnp.int32)
    keep_a, keep_b = keep[0:1], keep[1:2]

    block = clips.shape[1:]
    width = block[-1]
    *sends, cot_b = pack((clips, clips, cotangent), ((0,), (1,), (0,)), targets, whole=1)
    cot_b = spread(cot_b, groups)
    pieces = exchange(sends, size)
    cot_b = shuffle(cot_b, dest)
    weight_qkv, cot_b = lax.optimization_barrier((weight_qkv, cot_b))
    wt, wo = prepare(weight_qkv, weight_out)
    cot_b = spread(cot_b, groups).reshape(block)
    cot_b, wt = lax.optimization_barrier((cot_b, wt))
    out_a, out_b, *kept = forward(clips, pieces, origins, keep, wt, wo, scale)
    cot_b = lax.all_to_all(cot_b, "sp", 0, 0, tiled=True)
    cot_b, out_b = lax.optimization_barrier((cot_b, out_b))
    out_b = spread(out_b, groups)
    grad_a, grad_b = backward(cotangent[0], cot_b, pieces, origins, keep, wt, wo, kept, scale)
    grad_a, grad_b, out_a = grad_a.reshape(block), grad_b.reshape(block), out_a.reshape(block)
    out_b, grad_a = lax.optimization_barrier((out_b, grad_a))
    out_b = shuffle(out_b, source).reshape(groups * size, -1, width)
    out_b = lax.all_to_all(out_b, ("grp", "sp"), 0, 0, tiled=True).reshape(block)
    back = exchange(pack((grad_a, grad_b, out_a), (None, None, None), targets), size)
    grads, outputs = unpack((grad_a, grad_b, out_a, out_b), back, (0, 1, 2, None), origins)
    return (outputs, grads)


def solution(mesh):
    spec = P("grp", None, "sp", None)
    return jax.shard_map(
        on_device, mesh=mesh, in_specs=(spec, P(), P(), P(), P(), spec), out_specs=(spec, spec), check_vma=False
    )
```
